256 devices in a mesh: elem: 16 (over x_hi, y, core), freq: 16 (over x_lo, z).
Axes of the slice: x: 4 (x_hi: 2, x_lo: 2; x = x_hi * 2 + x_lo), y: 4, z: 8, core: 2. Of those that a mesh axis runs over, the one named last changes fastest.
Arguments:
- stress_modes: bfloat16 [3, 3000, 65536], P(None, None, ('elem', 'freq')), may hold values from -0.109375 to 0.109375
- node_shapes: float32 [4096, 3000], P(('elem', 'freq')), may hold values from -6 to 6
- wheel_nodes: int32 [4], replicated, may hold values from 0 to 4095
- mode_freq: float32 [3000], replicated, may hold values from 0.02 to 1.2
- mode_damping: float32 [3000], replicated, may hold values from 0.01 to 0.08
- freq_bins: int32 [384], P('freq'), may hold values from 1 to 4096
- delay_phase: int32 [4, 384], P(None, 'freq'), may hold values from 0 to 63
- road_psd: float32 [2, 384], P(None, 'freq'), may hold values from 0.05 to 1
- elem_block: int32 [65536], P(('elem', 'freq')), may hold values from 0 to 63
- block_scale: float32 [64], replicated, may hold values from 0.5 to 2
Outputs:
- spectra: bfloat16 [384, 9, 65536], P('freq', None, 'elem')
- moments: float32 [4, 65536], P(None, ('elem', 'freq'))
The draws below stay inside these ranges and needn't reach their ends.
All inputs are finite; a program needn't handle non-finite values.
Results may differ from the reference program's by a relative error of at most 0.0051.
Values may be sent and summed in bfloat16 or wider, within the bound.
A program may use at most 64 MiB of HBM per device.

```python
import math
import jax
import jax.numpy as jnp
from jax import lax

NM = 3000
E_DEV = 256
NBINS = 4096
PHASES = 64
NBLK = 64
NF = 384
ELEMS = 65536
NODES = 4096


def plant(drawn, stream_key, low, top_value):
    extent = drawn.shape
    index_at = [jax.random.randint(jax.random.fold_in(stream_key, axis), (), 0, extent[axis]) for axis in range(len(extent))]
    drawn = drawn.at[tuple(index_at)].set(low)
    longest = extent.index(max(extent))
    index_at[longest] = (index_at[longest] + 1) % extent[longest]
    return drawn.at[tuple(index_at)].set(top_value)


def shard_levels(rng, shape, pieces, smallest, high):
    gain, own = 1.0, jax.random.fold_in(rng, 6)
    for dim, blocks in pieces:
        draws = jnp.exp(jax.random.uniform(jax.random.fold_in(own, dim), (blocks,), jnp.float32, smallest / len(pieces), high / len(pieces)))
        gain = gain * jnp.repeat(draws, shape[dim] // blocks).reshape([-1 if axis == dim else 1 for axis in range(len(shape))])
    return gain


def normal_values(own_key, dims, width, limit, cuts=(), kind=jnp.bfloat16):
    result = jax.random.normal(own_key, dims, jnp.float32) * width
    if len(cuts) > 0:
        result = shard_levels(own_key, dims, cuts, -0.22, 0.18) * result
    return jnp.clip(result, min=-limit, max=limit).astype(kind)


def setup_inputs(seed: int = 0) -> dict:
    key_list = jax.random.split(jax.random.key(seed), 11)
    return {
        "stress_modes": normal_values(key_list[0], (3, NM, ELEMS), NM ** -0.5, 0.109375, ((2, 256),)),
        "node_shapes": normal_values(key_list[1], (NODES, NM), 1.0, 6.0, ((0, 256),), jnp.float32),
        "wheel_nodes": plant(jax.random.randint(key_list[2], (4,), 0, NODES), jax.random.fold_in(key_list[2], 1), 0, NODES - 1).astype(jnp.int32),
        "mode_freq": jnp.clip(jnp.exp(jax.random.uniform(key_list[3], (NM,), jnp.float32, math.log(0.02), math.log(1.2))), 0.02, 1.2),
        "mode_damping": jnp.clip(jnp.exp(jax.random.uniform(key_list[4], (NM,), jnp.float32, math.log(0.01), math.log(0.08))), 0.01, 0.08),
        "freq_bins": plant(jax.random.randint(key_list[5], (NF,), 1, NBINS + 1), jax.random.fold_in(key_list[5], 1), 1, NBINS).astype(jnp.int32),
        "delay_phase": plant(jax.random.randint(key_list[6], (4, NF), 0, PHASES), jax.random.fold_in(key_list[6], 1), 0, PHASES - 1).astype(jnp.int32),
        "road_psd": jnp.clip(jnp.exp(math.log(1.0) - 2.9957323 * jax.random.uniform(key_list[7], (2, NF), jnp.float32) ** shard_levels(key_list[7], (2, NF), ((1, 16),), -0.2, 0.2)), 0.05, 1.0),
        "elem_block": plant(jax.random.randint(key_list[8], (ELEMS,), 0, NBLK), jax.random.fold_in(key_list[8], 1), 0, NBLK - 1).astype(jnp.int32),
        "block_scale": jnp.clip(jnp.exp(jax.random.uniform(key_list[9], (NBLK,), jnp.float32, math.log(0.5), math.log(2.0))), 0.5, 2.0),
    }


def excitation(freq_bins, delay_phase, road_psd):
    line_ratio = freq_bins.astype(jnp.float32) / NBINS
    amplitude = jnp.repeat(jnp.sqrt(road_psd), 2, axis=0)
    angles = 2.0 * math.pi / PHASES * delay_phase.astype(jnp.float32)
    return jnp.concatenate([line_ratio[None, :], amplitude * jnp.cos(angles), amplitude * jnp.sin(angles)], axis=0)

def responses(factors, wheel_rows, mode_freq, mode_damping):
    line_ratio = factors[0][:, None]
    natural = mode_freq[None, :]
    detune = natural * natural - line_ratio * line_ratio
    damped = 2.0 * mode_damping[None, :] * natural * line_ratio
    magnitude = detune * detune + damped * damped
    gain_real = natural * natural * detune / magnitude
    gain_imag = -natural * natural * damped / magnitude
    columns = []
    for which_track in range(2):
        front_wheel = 2 * which_track
        rear_wheel = 2 * which_track + 1
        drive_real = factors[1 + front_wheel][:, None] * wheel_rows[front_wheel][None, :] + factors[1 + rear_wheel][:, None] * wheel_rows[rear_wheel][None, :]
        drive_imag = -(factors[5 + front_wheel][:, None] * wheel_rows[front_wheel][None, :] + factors[5 + rear_wheel][:, None] * wheel_rows[rear_wheel][None, :])
        columns.append(gain_real * drive_real - gain_imag * drive_imag)
        columns.append(gain_real * drive_imag + gain_imag * drive_real)
    return jnp.stack(columns, axis=1).astype(jnp.bfloat16)

def stress_scaling(elem_block, block_scale):
    matches = elem_block[None, :] == jnp.arange(block_scale.shape[0], dtype=jnp.int32)[:, None]
    return lax.optimization_barrier(jnp.sum(jnp.where(matches, block_scale[:, None], 0.0), axis=0))

def spectra_of(stress):
    real_part = stress[:, 0::2]
    imag_part = stress[:, 1::2]

    def cross_real(first_comp, second_comp):
        return lax.optimization_barrier(jnp.sum(real_part[:, :, first_comp] * real_part[:, :, second_comp] + imag_part[:, :, first_comp] * imag_part[:, :, second_comp], axis=1))

    def cross_imag(first_comp, second_comp):
        return lax.optimization_barrier(jnp.sum(imag_part[:, :, first_comp] * real_part[:, :, second_comp] - real_part[:, :, first_comp] * imag_part[:, :, second_comp], axis=1))
    return jnp.stack([cross_real(0, 0), cross_real(1, 1), cross_real(2, 2), cross_real(0, 1), cross_real(0, 2), cross_real(1, 2), cross_imag(0, 1), cross_imag(0, 2), cross_imag(1, 2)], axis=1)

def moments_of(spectrum, line_ratio):
    equivalent = spectrum[:, 0] + spectrum[:, 1] - spectrum[:, 3] + 3.0 * spectrum[:, 2]
    listed = [lax.optimization_barrier(jnp.sum((line_ratio ** exponent)[:, None] * equivalent, axis=0)) / line_ratio.shape[0] for exponent in (0, 1, 2, 4)]
    return jnp.stack(listed, axis=0)

def reference(stress_modes, node_shapes, wheel_nodes, mode_freq, mode_damping, freq_bins, delay_phase, road_psd, elem_block, block_scale):
    wheel_rows = node_shapes[wheel_nodes]
    factors = excitation(freq_bins, delay_phase, road_psd)
    modal = responses(factors, wheel_rows, mode_freq, mode_damping).astype(jnp.float32)
    scaling = stress_scaling(elem_block, block_scale)
    blocks = ELEMS // E_DEV
    spectra = jnp.zeros((NF, 9, ELEMS), jnp.bfloat16)
    moments = jnp.zeros((4, ELEMS), jnp.float32)

    def step_block(index, carry):
        spectra_now, moments_now = carry
        start = (index * E_DEV).astype(jnp.int32)
        panel = lax.dynamic_slice_in_dim(stress_modes, start, E_DEV, 2).astype(jnp.float32)
        factor_here = lax.dynamic_slice_in_dim(scaling, start, E_DEV, 0)
        stress = jnp.einsum('fkm,cme->fkce', modal, panel, precision=lax.Precision.HIGHEST) * factor_here
        spectrum = spectra_of(stress)
        spectra_now = lax.dynamic_update_slice_in_dim(spectra_now, spectrum.astype(jnp.bfloat16), start, 2)
        moments_now = lax.dynamic_update_slice_in_dim(moments_now, moments_of(spectrum, factors[0]), start, 1)
        return (spectra_now, moments_now)
    spectra, moments = lax.fori_loop(0, blocks, step_block, (spectra, moments))
    return (spectra, moments)
```

```python
import functools
import math

import jax
import jax.numpy as jnp
from jax import lax
from jax.experimental import pallas as pl
from jax.experimental.pallas import tpu as pltpu
from jax.sharding import PartitionSpec as P

NBINS = 4096
PHASES = 64
LANES = 128
PEERS = 16
MESH = pl.DeviceIdType.MESH


def partner(freq, step):
    across = 1 - step % 2
    rank = step // 2
    odd = rank % 2
    along = odd * (4 - (rank + 1) // 2) + (1 - odd) * (4 + rank // 2)
    x_lo, z = freq // 8, freq % 8
    return ((x_lo + across) % 2) * 8 + (z + along) % 8


def source(freq, step):
    across = 1 - step % 2
    rank = step // 2
    odd = rank % 2
    along = odd * (4 - (rank + 1) // 2) + (1 - odd) * (4 + rank // 2)
    x_lo, z = freq // 8, freq % 8
    return ((x_lo + across) % 2) * 8 + (z + 8 - along) % 8


def kernel(
    modes_any,
    shapes_any,
    nodes_any,
    natural_any,
    damping_any,
    bins_any,
    phase_any,
    road_any,
    block_any,
    scale_any,
    spectra_ref,
    moments_ref,
    modes,
    shapes,
    nodes,
    natural,
    damping,
    bins,
    phase,
    road,
    block,
    scale,
    picked,
    partial,
    summed,
    wheels,
    factors,
    scaling,
    modal,
    outgoing,
    arrived,
    spread,
    load_sem,
    send_a,
    recv_a,
    send_b,
    recv_b,
    send_c,
    recv_c,
    send_f,
    recv_f,
    send_s,
    recv_s,
):
    elem = lax.axis_index("elem")
    freq = lax.axis_index("freq")
    num_modes = natural.shape[1]
    lines = bins.shape[1]
    width = block.shape[1]
    tiles = -(-num_modes // LANES)
    rows_here = shapes.shape[0]

    barrier = pltpu.get_barrier_semaphore()

    def greet(step, carry):
        pl.semaphore_signal(barrier, inc=1, device_id=(elem, (freq + step) % PEERS), device_id_type=MESH)
        pl.semaphore_signal(barrier, inc=1, device_id=((elem + step) % PEERS, freq), device_id_type=MESH)
        return carry

    lax.fori_loop(1, PEERS, greet, 0)

    pairs = (
        (shapes_any, shapes),
        (nodes_any, nodes),
        (bins_any, bins),
        (phase_any, phase),
        (road_any, road),
        (natural_any, natural),
        (damping_any, damping),
        (block_any, block),
        (scale_any, scale),
        (modes_any, modes),
    )
    loads = [pltpu.make_async_copy(a, b, load_sem.at[i]) for i, (a, b) in enumerate(pairs)]
    for load in loads:
        load.start()
    for load in loads[:9]:
        load.wait()

    first_row = (elem * PEERS + freq) * rows_here
    row_number = lax.broadcasted_iota(jnp.int32, (rows_here, LANES), 0) + first_row
    masks = [row_number == nodes[:, w : w + 1] for w in range(4)]
    for t in range(tiles):
        lo, hi = t * LANES, min((t + 1) * LANES, num_modes)
        piece = shapes[:, lo:hi]
        found = [
            jnp.sum(jnp.where(m[:, : hi - lo], piece, 0.0), axis=0, keepdims=True) for m in masks
        ]
        picked[t // 2, (t % 2) * 4 : (t % 2) * 4 + 4, : hi - lo] = jnp.concatenate(found, axis=0)
    for j in range((tiles + 1) // 2, PEERS):
        picked[j] = jnp.zeros((8, LANES), jnp.float32)

    ratio = bins[...].astype(jnp.float32) / NBINS
    angle = 2.0 * math.pi / PHASES * phase[...].astype(jnp.float32)
    root = jnp.sqrt(road[...])
    amplitude = jnp.concatenate([root[0:1], root[0:1], root[1:2], root[1:2]], axis=0)
    table = jnp.concatenate(
        [
            ratio,
            amplitude * jnp.cos(angle),
            amplitude * jnp.sin(angle),
            jnp.zeros((LANES - 9, lines), jnp.float32),
        ],
        axis=0,
    )
    table = jnp.concatenate([table, jnp.zeros((LANES, LANES - lines), jnp.float32)], axis=1)
    factors[freq] = jnp.transpose(table)[:lines]

    pl.semaphore_wait(barrier, 2 * (PEERS - 1))

    def copy_a(step):
        peer = (elem + step) % PEERS
        return pltpu.make_async_remote_copy(
            src_ref=picked.at[peer],
            dst_ref=partial.at[step],
            send_sem=send_a.at[step],
            recv_sem=recv_a.at[step],
            device_id=(peer, freq),
            device_id_type=MESH,
        )

    def copy_f(step):
        return pltpu.make_async_remote_copy(
            src_ref=factors.at[freq],
            dst_ref=factors.at[freq],
            send_sem=send_f.at[step],
            recv_sem=recv_f.at[step],
            device_id=(elem, partner(freq, step)),
            device_id_type=MESH,
        )

    def copy_b(step):
        return pltpu.make_async_remote_copy(
            src_ref=summed.at[PEERS - 1],
            dst_ref=summed.at[step],
            send_sem=send_b.at[step],
            recv_sem=recv_b.at[step],
            device_id=(elem, partner(freq, step)),
            device_id_type=MESH,
        )

    def copy_c(step):
        return pltpu.make_async_remote_copy(
            src_ref=wheels.at[elem],
            dst_ref=wheels.at[elem],
            send_sem=send_c.at[step],
            recv_sem=recv_c.at[step],
            device_id=((elem + step) % PEERS, freq),
            device_id_type=MESH,
        )

    def started(copy, low, high):
        def body(step, carry):
            copy(step).start()
            return carry

        lax.fori_loop(low, high, body, 0)

    def received(copy, low, high):
        def body(step, carry):
            copy(step).wait_recv()
            return carry

        lax.fori_loop(low, high, body, 0)

    def sent(copy, low, high):
        def body(step, carry):
            copy(step).wait_send()
            return carry

        lax.fori_loop(low, high, body, 0)

    started(copy_a, 1, PEERS)
    started(copy_f, 0, PEERS - 1)
    partial[0] = picked[elem]

    sets = block[...]
    found = jnp.zeros(sets.shape, jnp.float32)
    for i in range(scale.shape[1]):
        found = jnp.where(sets == i, scale[:, i : i + 1], found)
    scaling[...] = found
    moments_ref[...] = jnp.zeros(moments_ref.shape, jnp.float32)

    received(copy_a, 1, PEERS)
    summed[PEERS - 1] = jnp.sum(partial[...], axis=0)
    started(copy_b, 0, PEERS - 1)
    received(copy_b, 0, PEERS - 1)
    wheels[elem] = jnp.sum(summed[...], axis=0)
    started(copy_c, 1, PEERS)
    loads[9].wait()
    received(copy_f, 0, PEERS - 1)
    received(copy_c, 1, PEERS)

    def copy_s(step):
        return pltpu.make_async_remote_copy(
            src_ref=outgoing.at[step],
            dst_ref=arrived.at[step],
            send_sem=send_s.at[step],
            recv_sem=recv_s.at[step],
            device_id=(elem, partner(freq, step)),
            device_id_type=MESH,
        )

    def serve(step, carry):
        table = factors[partner(freq, step)]
        column = [jnp.broadcast_to(table[:, i : i + 1], (lines, LANES)) for i in range(9)]
        square = column[0] * column[0]
        for t in range(tiles):
            lo, hi = t * LANES, min((t + 1) * LANES, num_modes)
            size = hi - lo
            v = natural[:, lo:hi]
            z = damping[:, lo:hi]
            w = [wheels[t // 2, (t % 2) * 4 + i : (t % 2) * 4 + i + 1, :size] for i in range(4)]
            col = [c[:, :size] for c in column]
            own = v * v
            detune = own - square[:, :size]
            damped = (2.0 * z * v) * col[0]
            gain = own / (detune * detune + damped * damped)
            gain_real = gain * detune
            gain_imag = gain * damped
            for k in range(2):
                real = col[1 + 2 * k] * w[2 * k] + col[2 + 2 * k] * w[2 * k + 1]
                imag = col[5 + 2 * k] * w[2 * k] + col[6 + 2 * k] * w[2 * k + 1]
                both = jnp.concatenate(
                    [
                        gain_real * real - gain_imag * imag,
                        -(gain_real * imag + gain_imag * real),
                    ],
                    axis=0,
                )
                modal[2 * k * lines : 2 * (k + 1) * lines, lo:hi] = both.astype(jnp.bfloat16)
        factor = scaling[...]
        stress = []
        for c in range(3):
            product = jnp.dot(modal[...], modes[c], preferred_element_type=jnp.float32) * factor
            stress.append([product[k * lines : (k + 1) * lines] for k in range(4)])

        def real_of(a, b):
            a, b = stress[a], stress[b]
            return a[0] * b[0] + a[1] * b[1] + (a[2] * b[2] + a[3] * b[3])

        def imag_of(a, b):
            a, b = stress[a], stress[b]
            return a[1] * b[0] - a[0] * b[1] + (a[3] * b[2] - a[2] * b[3])

        cross = [
            real_of(0, 0),
            real_of(1, 1),
            real_of(2, 2),
            real_of(0, 1),
            real_of(0, 2),
            real_of(1, 2),
            imag_of(0, 1),
            imag_of(0, 2),
            imag_of(1, 2),
        ]
        for i, value in enumerate(cross):
            halves = jnp.concatenate([value[:, :LANES], value[:, LANES:]], axis=0)
            outgoing[step, i] = halves.astype(jnp.bfloat16)

        @pl.when(step < PEERS - 1)
        def _():
            copy_s(step).start()

        equivalent = cross[0] + cross[1] - cross[3] + 3.0 * cross[2]
        r = table[:, 0:1]
        r2 = r * r
        listed = [
            jnp.sum(value, axis=0, keepdims=True)
            for value in (equivalent, r * equivalent, r2 * equivalent, (r2 * r2) * equivalent)
        ]
        moments_ref[...] += jnp.concatenate(listed, axis=0)
        return carry

    lax.fori_loop(0, PEERS, serve, 0)
    moments_ref[...] = moments_ref[...] / (PEERS * lines)

    def place(ref, step):
        start = source(freq, step) * width
        for half in range(2):
            for i in range(9):
                value = ref[i, half * lines : (half + 1) * lines].astype(jnp.float32)
                spread[half, pl.ds(i, lines, stride=16), :] = value
            at = pl.multiple_of(start + half * LANES, LANES)
            for f in range(lines):
                spectra_ref[f, :, pl.ds(at, LANES)] = spread[half, f * 16 : f * 16 + 9, :].astype(
                    jnp.bfloat16
                )

    place(outgoing.at[PEERS - 1], PEERS - 1)

    def take(step, carry):
        copy_s(step).wait_recv()
        place(arrived.at[step], step)
        return carry

    lax.fori_loop(0, PEERS - 1, take, 0)
    sent(copy_a, 1, PEERS)
    sent(copy_f, 0, PEERS - 1)
    sent(copy_b, 0, PEERS - 1)
    sent(copy_c, 1, PEERS)
    sent(copy_s, 0, PEERS - 1)


def local(*args):
    modes, shapes, nodes, natural, damping, bins, phase, road, block, scale = args
    row = [a.reshape(1, -1) for a in (nodes, natural, damping, bins)]
    args = (modes, shapes, *row, phase, road, block.reshape(1, -1), scale.reshape(1, -1))
    num_modes, width = modes.shape[1:]
    lines = bins.shape[0]
    f32, bf16 = jnp.float32, jnp.bfloat16
    sems = pltpu.SemaphoreType.DMA((PEERS,))
    return pl.pallas_call(
        kernel,
        out_shape=(
            jax.ShapeDtypeStruct((lines, 9, PEERS * width), bf16),
            jax.ShapeDtypeStruct((4, width), f32),
        ),
        in_specs=[pl.BlockSpec(memory_space=pl.ANY)] * len(args),
        out_specs=(pl.BlockSpec(memory_space=pltpu.VMEM),) * 2,
        scratch_shapes=[
            *[pltpu.VMEM(a.shape, a.dtype) for a in args],
            pltpu.VMEM((PEERS, 8, LANES), f32),
            pltpu.VMEM((PEERS, 8, LANES), f32),
            pltpu.VMEM((PEERS, 8, LANES), f32),
            pltpu.VMEM((PEERS, 8, LANES), f32),
            pltpu.VMEM((PEERS, lines, LANES), f32),
            pltpu.VMEM((1, width), f32),
            pltpu.VMEM((4 * lines, num_modes), bf16),
            pltpu.VMEM((PEERS, 9, 2 * lines, LANES), bf16),
            pltpu.VMEM((PEERS, 9, 2 * lines, LANES), bf16),
            pltpu.VMEM((2, 16 * lines, LANES), f32),
            sems,
            *[sems] * 10,
        ],
        compiler_params=pltpu.CompilerParams(
            collective_id=0, has_side_effects=True, vmem_limit_bytes=40 << 20
        ),
        cost_estimate=pl.CostEstimate(flops=7_100_000_000, bytes_accessed=10_000_000, transcendentals=0),
    )(*args)


def solution(mesh):
    placed = (
        P(None, None, ("elem", "freq")),
        P(("elem", "freq"), None),
        P(),
        P(),
        P(),
        P("freq"),
        P(None, "freq"),
        P(None, "freq"),
        P(("elem", "freq")),
        P(),
    )
    return jax.shard_map(
        local,
        mesh=mesh,
        in_specs=placed,
        out_specs=(P("freq", None, "elem"), P(None, ("elem", "freq"))),
        check_vma=False,
    )
```

```python
import functools
import math

import jax
import jax.numpy as jnp
from jax import lax
from jax.experimental import pallas as pl
from jax.experimental.pallas import tpu as pltpu
from jax.sharding import PartitionSpec as P

NBINS = 4096
PHASES = 64
LANES = 128
PEERS = 16
MESH = pl.DeviceIdType.MESH


def partner(freq, step):
    across = 1 - step % 2
    rank = step // 2
    odd = rank % 2
    along = odd * (4 - (rank + 1) // 2) + (1 - odd) * (4 + rank // 2)
    x_lo, z = freq // 8, freq % 8
    return ((x_lo + across) % 2) * 8 + (z + along) % 8


ELEM_STEPS = [(x, y, c) for y in (2, 1, 3, 0) for x in (1, 0) for c in (1, 0)][:-1]


def elem_peer(elem, step):
    x, y, c = ELEM_STEPS[step]
    x_hi, y_at, core = elem // 8, (elem // 2) % 4, elem % 2
    return ((x_hi + x) % 2) * 8 + ((y_at + y) % 4) * 2 + (core + c) % 2


def kernel(
    modes_any,
    shapes_any,
    nodes_any,
    natural_any,
    damping_any,
    bins_any,
    phase_any,
    road_any,
    block_any,
    scale_any,
    spectra_ref,
    moments_ref,
    modes,
    shapes,
    nodes,
    natural,
    damping,
    bins,
    phase,
    road,
    block,
    scale,
    picked,
    partial,
    summed,
    wheels,
    factors,
    scaling,
    modal,
    outgoing,
    load_sem,
    send_a,
    recv_a,
    send_b,
    recv_b,
    send_c,
    recv_c,
    send_f,
    recv_f,
    send_s,
    recv_s,
):
    elem = lax.axis_index("elem")
    freq = lax.axis_index("freq")
    num_modes = natural.shape[1]
    lines = bins.shape[1]
    width = block.shape[1]
    tiles = -(-num_modes // LANES)
    rows_here = shapes.shape[0]

    barrier = pltpu.get_barrier_semaphore()

    for step in range(PEERS - 1):
        for peer in ((elem, partner(freq, step)), (elem_peer(elem, step), freq)):
            pl.semaphore_signal(barrier, inc=1, device_id=peer, device_id_type=MESH)

    pairs = (
        (shapes_any, shapes),
        (nodes_any, nodes),
        (bins_any, bins),
        (phase_any, phase),
        (road_any, road),
        (natural_any, natural),
        (damping_any, damping),
        (block_any, block),
        (scale_any, scale),
        (modes_any, modes),
    )
    loads = [pltpu.make_async_copy(a, b, load_sem.at[i]) for i, (a, b) in enumerate(pairs)]
    for load in loads:
        load.start()
    for load in loads[:9]:
        load.wait()

    first_row = (elem * PEERS + freq) * rows_here
    row_number = lax.broadcasted_iota(jnp.int32, (rows_here, LANES), 0) + first_row
    masks = [row_number == nodes[:, w : w + 1] for w in range(4)]
    for t in range(tiles):
        lo, hi = t * LANES, min((t + 1) * LANES, num_modes)
        piece = shapes[:, lo:hi]
        found = [
            jnp.sum(jnp.where(m[:, : hi - lo], piece, 0.0), axis=0, keepdims=True) for m in masks
        ]
        picked[t // 2, (t % 2) * 4 : (t % 2) * 4 + 4, : hi - lo] = jnp.concatenate(found, axis=0)
    for j in range((tiles + 1) // 2, PEERS):
        picked[j] = jnp.zeros((8, LANES), jnp.float32)

    ratio = bins[...].astype(jnp.float32) / NBINS
    angle = 2.0 * math.pi / PHASES * phase[...].astype(jnp.float32)
    root = jnp.sqrt(road[...])
    amplitude = jnp.concatenate([root[0:1], root[0:1], root[1:2], root[1:2]], axis=0)
    table = jnp.concatenate(
        [
            ratio,
            amplitude * jnp.cos(angle),
            amplitude * jnp.sin(angle),
            jnp.zeros((LANES - 9, lines), jnp.float32),
        ],
        axis=0,
    )
    table = jnp.concatenate([table, jnp.zeros((LANES, LANES - lines), jnp.float32)], axis=1)
    factors[freq] = jnp.transpose(table)[:lines]

    pl.semaphore_wait(barrier, 2 * (PEERS - 1))

    def copy_a(step):
        peer = elem_peer(elem, step)
        return pltpu.make_async_remote_copy(
            src_ref=picked.at[peer],
            dst_ref=partial.at[step],
            send_sem=send_a.at[step],
            recv_sem=recv_a.at[step],
            device_id=(peer, freq),
            device_id_type=MESH,
        )

    def copy_f(step):
        return pltpu.make_async_remote_copy(
            src_ref=factors.at[freq],
            dst_ref=factors.at[freq],
            send_sem=send_f.at[step],
            recv_sem=recv_f.at[step],
            device_id=(elem, partner(freq, step)),
            device_id_type=MESH,
        )

    def copy_b(step):
        return pltpu.make_async_remote_copy(
            src_ref=summed.at[PEERS - 1],
            dst_ref=summed.at[step],
            send_sem=send_b.at[step],
            recv_sem=recv_b.at[step],
            device_id=(elem, partner(freq, step)),
            device_id_type=MESH,
        )

    def copy_c(step):
        return pltpu.make_async_remote_copy(
            src_ref=wheels.at[elem],
            dst_ref=wheels.at[elem],
            send_sem=send_c.at[step],
            recv_sem=recv_c.at[step],
            device_id=(elem_peer(elem, step), freq),
            device_id_type=MESH,
        )

    def started(copy):
        for step in range(PEERS - 1):
            copy(step).start()

    def received(copy):
        for step in range(PEERS - 1):
            copy(step).wait_recv()

    def sent(copy):
        for step in range(PEERS - 1):
            copy(step).wait_send()

    started(copy_a)
    started(copy_f)
    partial[PEERS - 1] = picked[elem]

    sets = block[...]
    found = jnp.zeros(sets.shape, jnp.float32)
    for i in range(scale.shape[1]):
        found = jnp.where(sets == i, scale[:, i : i + 1], found)
    scaling[...] = found
    moments_ref[...] = jnp.zeros(moments_ref.shape, jnp.float32)

    received(copy_a)
    summed[PEERS - 1] = jnp.sum(partial[...], axis=0)
    started(copy_b)
    received(copy_b)
    wheels[elem] = jnp.sum(summed[...], axis=0)
    started(copy_c)
    loads[9].wait()
    received(copy_f)
    received(copy_c)

    here = pl.ds(pl.multiple_of(freq * width, width), width)

    def copy_s(step):
        return pltpu.make_async_remote_copy(
            src_ref=outgoing.at[step],
            dst_ref=spectra_ref.at[:, :, here],
            send_sem=send_s.at[step],
            recv_sem=recv_s.at[step],
            device_id=(elem, partner(freq, step)),
            device_id_type=MESH,
        )

    def serve(step, carry):
        table = factors[partner(freq, step)]
        column = [jnp.broadcast_to(table[:, i : i + 1], (lines, LANES)) for i in range(9)]
        square = column[0] * column[0]
        for t in range(tiles):
            lo, hi = t * LANES, min((t + 1) * LANES, num_modes)
            size = hi - lo
            v = natural[:, lo:hi]
            z = damping[:, lo:hi]
            w = [wheels[t // 2, (t % 2) * 4 + i : (t % 2) * 4 + i + 1, :size] for i in range(4)]
            col = [c[:, :size] for c in column]
            own = v * v
            detune = own - square[:, :size]
            damped = (2.0 * z * v) * col[0]
            gain = own / (detune * detune + damped * damped)
            gain_real = gain * detune
            gain_imag = gain * damped
            for k in range(2):
                real = col[1 + 2 * k] * w[2 * k] + col[2 + 2 * k] * w[2 * k + 1]
                imag = col[5 + 2 * k] * w[2 * k] + col[6 + 2 * k] * w[2 * k + 1]
                both = jnp.concatenate(
                    [
                        gain_real * real - gain_imag * imag,
                        -(gain_real * imag + gain_imag * real),
                    ],
                    axis=0,
                )
                modal[2 * k * lines : 2 * (k + 1) * lines, lo:hi] = both.astype(jnp.bfloat16)
        factor = scaling[...]
        stress = []
        for c in range(3):
            product = jnp.dot(modal[...], modes[c], preferred_element_type=jnp.float32) * factor
            stress.append([product[k * lines : (k + 1) * lines] for k in range(4)])

        def real_of(a, b):
            a, b = stress[a], stress[b]
            return a[0] * b[0] + a[1] * b[1] + (a[2] * b[2] + a[3] * b[3])

        def imag_of(a, b):
            a, b = stress[a], stress[b]
            return a[1] * b[0] - a[0] * b[1] + (a[3] * b[2] - a[2] * b[3])

        cross = [
            real_of(0, 0),
            real_of(1, 1),
            real_of(2, 2),
            real_of(0, 1),
            real_of(0, 2),
            real_of(1, 2),
            imag_of(0, 1),
            imag_of(0, 2),
            imag_of(1, 2),
        ]
        for i, value in enumerate(cross):
            outgoing[step, i] = value.astype(jnp.bfloat16)

        @pl.when(step < PEERS - 1)
        def _():
            copy_s(step).start()

        equivalent = cross[0] + cross[1] - cross[3] + 3.0 * cross[2]
        r = table[:, 0:1]
        r2 = r * r
        listed = [
            jnp.sum(value, axis=0, keepdims=True)
            for value in (equivalent, r * equivalent, r2 * equivalent, (r2 * r2) * equivalent)
        ]
        moments_ref[...] += jnp.concatenate(listed, axis=0)
        return carry

    lax.fori_loop(0, PEERS, serve, 0)
    moments_ref[...] = moments_ref[...] / (PEERS * lines)

    keep = pltpu.make_async_copy(outgoing.at[PEERS - 1], spectra_ref.at[:, :, here], load_sem.at[0])
    keep.start()
    for step in range(PEERS - 1):
        copy_s(step).wait_recv()
    keep.wait()
    for copy in (copy_a, copy_f, copy_b, copy_c, copy_s):
        sent(copy)


def local(*args):
    modes, shapes, nodes, natural, damping, bins, phase, road, block, scale = args
    row = [a.reshape(1, -1) for a in (nodes, natural, damping, bins)]
    args = (modes, shapes, *row, phase, road, block.reshape(1, -1), scale.reshape(1, -1))
    args = [pltpu.with_memory_space_constraint(a, pltpu.HBM) for a in args]
    num_modes, width = modes.shape[1:]
    lines = bins.shape[0]
    f32, bf16 = jnp.float32, jnp.bfloat16
    sems = pltpu.SemaphoreType.DMA((PEERS,))
    spectra, moments = pl.pallas_call(
        kernel,
        out_shape=(
            jax.ShapeDtypeStruct((9, lines, PEERS * width), bf16),
            jax.ShapeDtypeStruct((4, width), f32),
        ),
        in_specs=[pl.BlockSpec(memory_space=pltpu.HBM)] * len(args),
        out_specs=(pl.BlockSpec(memory_space=pltpu.VMEM),) * 2,
        scratch_shapes=[
            *[pltpu.VMEM(a.shape, a.dtype) for a in args],
            pltpu.VMEM((PEERS, 8, LANES), f32),
            pltpu.VMEM((PEERS, 8, LANES), f32),
            pltpu.VMEM((PEERS, 8, LANES), f32),
            pltpu.VMEM((PEERS, 8, LANES), f32),
            pltpu.VMEM((PEERS, lines, LANES), f32),
            pltpu.VMEM((1, width), f32),
            pltpu.VMEM((4 * lines, num_modes), bf16),
            pltpu.VMEM((PEERS, 9, lines, width), bf16),
            sems,
            *[sems] * 10,
        ],
        compiler_params=pltpu.CompilerParams(
            collective_id=0, has_side_effects=True, vmem_limit_bytes=40 << 20
        ),
        cost_estimate=pl.CostEstimate(flops=7_100_000_000, bytes_accessed=10_000_000, transcendentals=0),
    )(*args)
    return jnp.transpose(spectra, (1, 0, 2)), moments


def solution(mesh):
    placed = (
        P(None, None, ("elem", "freq")),
        P(("elem", "freq"), None),
        P(),
        P(),
        P(),
        P("freq"),
        P(None, "freq"),
        P(None, "freq"),
        P(("elem", "freq")),
        P(),
    )
    return jax.shard_map(
        local,
        mesh=mesh,
        in_specs=placed,
        out_specs=(P("freq", None, "elem"), P(None, ("elem", "freq"))),
        check_vma=False,
    )
```

```python
import functools
import math

import jax
import jax.numpy as jnp
from jax import lax
from jax.experimental import pallas as pl
from jax.experimental.pallas import tpu as pltpu
from jax.sharding import PartitionSpec as P

NBINS = 4096
PHASES = 64
LANES = 128
PEERS = 16
MESH = pl.DeviceIdType.MESH


def partner(freq, step):
    across = 1 - step % 2
    rank = step // 2
    odd = rank % 2
    along = odd * (4 - (rank + 1) // 2) + (1 - odd) * (4 + rank // 2)
    x_lo, z = freq // 8, freq % 8
    return ((x_lo + across) % 2) * 8 + (z + along) % 8


def source(freq, step):
    across = 1 - step % 2
    rank = step // 2
    odd = rank % 2
    along = odd * (4 - (rank + 1) // 2) + (1 - odd) * (4 + rank // 2)
    x_lo, z = freq // 8, freq % 8
    return ((x_lo + across) % 2) * 8 + (z + 8 - along) % 8


def unit(parts):
    top = jnp.abs(parts[0])
    for part in parts[1:]:
        top = jnp.maximum(top, jnp.abs(part))
    some = top > 1e-37
    scaled = [part * (1.0 / jnp.where(some, top, 1.0)) for part in parts]
    total = scaled[0] * scaled[0]
    for part in scaled[1:]:
        total += part * part
    shrink = lax.rsqrt(jnp.where(some, total, 1.0))
    direction = [jnp.where(some, part * shrink, 1.0 if i == 0 else 0.0) for i, part in enumerate(scaled)]
    return direction, jnp.where(some, top * (total * shrink), 0.0)


ELEM_STEPS = [(x, y, c) for y in (2, 1, 3, 0) for x in (1, 0) for c in (1, 0)][:-1]


def elem_peer(elem, step):
    x, y, c = ELEM_STEPS[step]
    x_hi, y_at, core = elem // 8, (elem // 2) % 4, elem % 2
    return ((x_hi + x) % 2) * 8 + ((y_at + y) % 4) * 2 + (core + c) % 2


def kernel(
    modes_any,
    shapes_any,
    nodes_any,
    natural_any,
    damping_any,
    bins_any,
    phase_any,
    road_any,
    block_any,
    scale_any,
    spectra_ref,
    moments_ref,
    modes,
    shapes,
    nodes,
    natural,
    damping,
    bins,
    phase,
    road,
    block,
    scale,
    picked,
    partial,
    summed,
    wheels,
    factors,
    scaling,
    modal,
    outgoing,
    arrived,
    load_sem,
    send_a,
    recv_a,
    send_b,
    recv_b,
    send_c,
    recv_c,
    send_s,
    recv_s,
):
    elem = lax.axis_index("elem")
    freq = lax.axis_index("freq")
    num_modes = natural.shape[1]
    lines = bins.shape[1]
    width = block.shape[1]
    tiles = -(-num_modes // LANES)
    rows_here = shapes.shape[0]

    barrier = pltpu.get_barrier_semaphore()

    for step in range(PEERS - 1):
        for peer in ((elem, partner(freq, step)), (elem_peer(elem, step), freq)):
            pl.semaphore_signal(barrier, inc=1, device_id=peer, device_id_type=MESH)

    pairs = (
        (shapes_any, shapes),
        (nodes_any, nodes),
        (bins_any, bins),
        (phase_any, phase),
        (road_any, road),
        (natural_any, natural),
        (damping_any, damping),
        (block_any, block),
        (scale_any, scale),
        (modes_any, modes),
    )
    loads = [pltpu.make_async_copy(a, b, load_sem.at[i]) for i, (a, b) in enumerate(pairs)]
    for load in loads:
        load.start()
    for load in loads[:9]:
        load.wait()

    first_row = (elem * PEERS + freq) * rows_here
    row_number = lax.broadcasted_iota(jnp.int32, (rows_here, LANES), 0) + first_row
    masks = [row_number == nodes[:, w : w + 1] for w in range(4)]
    for t in range(tiles):
        lo, hi = t * LANES, min((t + 1) * LANES, num_modes)
        piece = shapes[:, lo:hi]
        found = [
            jnp.sum(jnp.where(m[:, : hi - lo], piece, 0.0), axis=0, keepdims=True) for m in masks
        ]
        picked[t // 2, (t % 2) * 4 : (t % 2) * 4 + 4, : hi - lo] = jnp.concatenate(found, axis=0)
    for j in range((tiles + 1) // 2, PEERS):
        picked[j] = jnp.zeros((8, LANES), jnp.float32)

    ratio = bins[...].astype(jnp.float32) / NBINS
    angle = 2.0 * math.pi / PHASES * phase[...].astype(jnp.float32)
    root = jnp.sqrt(road[...])
    amplitude = jnp.concatenate([root[0:1], root[0:1], root[1:2], root[1:2]], axis=0)
    waves = jnp.concatenate([amplitude * jnp.cos(angle), amplitude * jnp.sin(angle)], axis=0)
    ratios = jnp.concatenate([ratio, jnp.zeros((7, lines), jnp.float32)], axis=0)
    rest = jnp.zeros((8, LANES - 2 * lines), jnp.float32)
    summed[PEERS - 1, 8:] = jnp.concatenate([waves, ratios, rest], axis=1)

    pl.semaphore_wait(barrier, 2 * (PEERS - 1))

    def copy_a(step):
        peer = elem_peer(elem, step)
        return pltpu.make_async_remote_copy(
            src_ref=picked.at[peer],
            dst_ref=partial.at[step],
            send_sem=send_a.at[step],
            recv_sem=recv_a.at[step],
            device_id=(peer, freq),
            device_id_type=MESH,
        )

    def copy_b(step):
        return pltpu.make_async_remote_copy(
            src_ref=summed.at[PEERS - 1],
            dst_ref=summed.at[step],
            send_sem=send_b.at[step],
            recv_sem=recv_b.at[step],
            device_id=(elem, partner(freq, step)),
            device_id_type=MESH,
        )

    def copy_c(step):
        return pltpu.make_async_remote_copy(
            src_ref=wheels.at[elem],
            dst_ref=wheels.at[elem],
            send_sem=send_c.at[step],
            recv_sem=recv_c.at[step],
            device_id=(elem_peer(elem, step), freq),
            device_id_type=MESH,
        )

    def started(copy):
        for step in range(PEERS - 1):
            copy(step).start()

    def received(copy):
        for step in range(PEERS - 1):
            copy(step).wait_recv()

    def sent(copy):
        for step in range(PEERS - 1):
            copy(step).wait_send()

    started(copy_a)
    partial[PEERS - 1] = picked[elem]

    sets = block[...]
    found = jnp.zeros(sets.shape, jnp.float32)
    for i in range(scale.shape[1]):
        found = jnp.where(sets == i, scale[:, i : i + 1], found)
    scaling[...] = found
    moments_ref[...] = jnp.zeros(moments_ref.shape, jnp.float32)

    received(copy_a)
    summed[PEERS - 1, :8] = jnp.sum(partial[...], axis=0)
    started(copy_b)
    received(copy_b)
    wheels[elem] = jnp.sum(summed[:, :8], axis=0)
    started(copy_c)
    for step in range(PEERS):
        factors[source(freq, step)] = jnp.transpose(summed[step, 8:])[: 2 * lines]
    loads[9].wait()
    received(copy_c)

    def copy_s(step):
        return pltpu.make_async_remote_copy(
            src_ref=outgoing.at[step],
            dst_ref=arrived.at[step],
            send_sem=send_s.at[step],
            recv_sem=recv_s.at[step],
            device_id=(elem, partner(freq, step)),
            device_id_type=MESH,
        )

    def serve(step, carry):
        table = factors[partner(freq, step)]
        r = table[lines:, 0:1]
        column = [r] + [table[:lines, i : i + 1] for i in range(8)]
        column = [jnp.broadcast_to(c, (lines, LANES)) for c in column]
        square = column[0] * column[0]
        for t in range(tiles):
            lo, hi = t * LANES, min((t + 1) * LANES, num_modes)
            size = hi - lo
            v = natural[:, lo:hi]
            z = damping[:, lo:hi]
            w = [wheels[t // 2, (t % 2) * 4 + i : (t % 2) * 4 + i + 1, :size] for i in range(4)]
            col = [c[:, :size] for c in column]
            own = v * v
            detune = own - square[:, :size]
            damped = (2.0 * z * v) * col[0]
            gain = own / (detune * detune + damped * damped)
            gain_real = gain * detune
            gain_imag = gain * damped
            for k in range(2):
                real = col[1 + 2 * k] * w[2 * k] + col[2 + 2 * k] * w[2 * k + 1]
                imag = col[5 + 2 * k] * w[2 * k] + col[6 + 2 * k] * w[2 * k + 1]
                both = jnp.concatenate(
                    [
                        gain_real * real - gain_imag * imag,
                        -(gain_real * imag + gain_imag * real),
                    ],
                    axis=0,
                )
                modal[2 * k * lines : 2 * (k + 1) * lines, lo:hi] = both.astype(jnp.bfloat16)
        factor = scaling[...]
        stress = []
        for c in range(3):
            product = jnp.dot(modal[...], modes[c], preferred_element_type=jnp.float32) * factor
            stress.append([product[k * lines : (k + 1) * lines] for k in range(4)])

        def real_of(a, b):
            return a[0] * b[0] + a[1] * b[1] + (a[2] * b[2] + a[3] * b[3])

        def imag_of(a, b):
            return a[1] * b[0] - a[0] * b[1] + (a[3] * b[2] - a[2] * b[3])

        def off_real(a, n):
            return a[2] * n[0] - a[3] * n[1] - (a[0] * n[2] - a[1] * n[3])

        def off_imag(a, n):
            return a[2] * n[1] + a[3] * n[0] - (a[0] * n[3] + a[1] * n[2])

        first, second, third = stress
        along, length = unit(first)
        turn, height = unit([off_real(second, along), off_imag(second, along)])
        x, y = off_real(third, along), off_imag(third, along)
        triangle = [
            length,
            real_of(second, along),
            imag_of(second, along),
            real_of(third, along),
            imag_of(third, along),
            height,
            x * turn[0] + y * turn[1],
            y * turn[0] - x * turn[1],
        ]
        for i, value in enumerate(triangle):
            outgoing[step, i] = value.astype(jnp.bfloat16)

        @pl.when(step < PEERS - 1)
        def _():
            copy_s(step).start()

        equivalent = (
            real_of(first, first)
            + real_of(second, second)
            - real_of(first, second)
            + 3.0 * real_of(third, third)
        )
        r2 = r * r
        listed = [
            jnp.sum(value, axis=0, keepdims=True)
            for value in (equivalent, r * equivalent, r2 * equivalent, (r2 * r2) * equivalent)
        ]
        moments_ref[...] += jnp.concatenate(listed, axis=0)
        return carry

    lax.fori_loop(0, PEERS, serve, 0)
    moments_ref[...] = moments_ref[...] / (PEERS * lines)

    def expand(ref, step):
        at = pl.ds(pl.multiple_of(source(freq, step) * width, width), width)
        r, br, bi, cr, ci, h, dr, di = (ref[i].astype(jnp.float32) for i in range(8))
        cross = (
            r * r,
            br * br + bi * bi + h * h,
            cr * cr + ci * ci + (dr * dr + di * di),
            r * br,
            r * cr,
            br * cr + bi * ci + h * dr,
            -(r * bi),
            -(r * ci),
            bi * cr - br * ci - h * di,
        )
        for i, value in enumerate(cross):
            spectra_ref[i, :, at] = value.astype(jnp.bfloat16)

    expand(outgoing.at[PEERS - 1], PEERS - 1)

    def take(step, carry):
        copy_s(step).wait_recv()
        expand(arrived.at[step], step)
        return carry

    lax.fori_loop(0, PEERS - 1, take, 0)
    for copy in (copy_a, copy_b, copy_c, copy_s):
        sent(copy)


def local(*args):
    modes, shapes, nodes, natural, damping, bins, phase, road, block, scale = args
    row = [a.reshape(1, -1) for a in (nodes, natural, damping, bins)]
    args = (modes, shapes, *row, phase, road, block.reshape(1, -1), scale.reshape(1, -1))
    args = [pltpu.with_memory_space_constraint(a, pltpu.HBM) for a in args]
    num_modes, width = modes.shape[1:]
    lines = bins.shape[0]
    f32, bf16 = jnp.float32, jnp.bfloat16
    sems = pltpu.SemaphoreType.DMA((PEERS,))
    spectra, moments = pl.pallas_call(
        kernel,
        out_shape=(
            jax.ShapeDtypeStruct((9, lines, PEERS * width), bf16),
            jax.ShapeDtypeStruct((4, width), f32),
        ),
        in_specs=[pl.BlockSpec(memory_space=pltpu.HBM)] * len(args),
        out_specs=(pl.BlockSpec(memory_space=pltpu.VMEM),) * 2,
        scratch_shapes=[
            *[pltpu.VMEM(a.shape, a.dtype) for a in args],
            pltpu.VMEM((PEERS, 8, LANES), f32),
            pltpu.VMEM((PEERS, 8, LANES), f32),
            pltpu.VMEM((PEERS, 16, LANES), f32),
            pltpu.VMEM((PEERS, 8, LANES), f32),
            pltpu.VMEM((PEERS, 2 * lines, 8), f32),
            pltpu.VMEM((1, width), f32),
            pltpu.VMEM((4 * lines, num_modes), bf16),
            pltpu.VMEM((PEERS, 8, lines, width), bf16),
            pltpu.VMEM((PEERS, 8, lines, width), bf16),
            sems,
            *[sems] * 8,
        ],
        compiler_params=pltpu.CompilerParams(
            collective_id=0, has_side_effects=True, vmem_limit_bytes=40 << 20
        ),
        cost_estimate=pl.CostEstimate(flops=7_100_000_000, bytes_accessed=10_000_000, transcendentals=0),
    )(*args)
    return jnp.transpose(spectra, (1, 0, 2)), moments


def solution(mesh):
    placed = (
        P(None, None, ("elem", "freq")),
        P(("elem", "freq"), None),
        P(),
        P(),
        P(),
        P("freq"),
        P(None, "freq"),
        P(None, "freq"),
        P(("elem", "freq")),
        P(),
    )
    return jax.shard_map(
        local,
        mesh=mesh,
        in_specs=placed,
        out_specs=(P("freq", None, "elem"), P(None, ("elem", "freq"))),
        check_vma=False,
    )
```

```python
import functools
import math

import jax
import jax.numpy as jnp
from jax import lax
from jax.experimental import pallas as pl
from jax.experimental.pallas import tpu as pltpu
from jax.sharding import PartitionSpec as P

NBINS = 4096
PHASES = 64
LANES = 128
PEERS = 16
MESH = pl.DeviceIdType.MESH


def partner(freq, step):
    across = 1 - step % 2
    rank = step // 2
    odd = rank % 2
    along = odd * (4 - (rank + 1) // 2) + (1 - odd) * (4 + rank // 2)
    x_lo, z = freq // 8, freq % 8
    return ((x_lo + across) % 2) * 8 + (z + along) % 8


def source(freq, step):
    across = 1 - step % 2
    rank = step // 2
    odd = rank % 2
    along = odd * (4 - (rank + 1) // 2) + (1 - odd) * (4 + rank // 2)
    x_lo, z = freq // 8, freq % 8
    return ((x_lo + across) % 2) * 8 + (z + 8 - along) % 8


def unit(parts):
    top = jnp.abs(parts[0])
    for part in parts[1:]:
        top = jnp.maximum(top, jnp.abs(part))
    some = top > 1e-37
    scaled = [part * (1.0 / jnp.where(some, top, 1.0)) for part in parts]
    total = scaled[0] * scaled[0]
    for part in scaled[1:]:
        total += part * part
    shrink = lax.rsqrt(jnp.where(some, total, 1.0))
    direction = [jnp.where(some, part * shrink, 1.0 if i == 0 else 0.0) for i, part in enumerate(scaled)]
    return direction, jnp.where(some, top * (total * shrink), 0.0)


ELEM_STEPS = [(x, y, c) for y in (2, 1, 3, 0) for x in (1, 0) for c in (1, 0)][:-1]


def elem_peer(elem, step):
    x, y, c = ELEM_STEPS[step]
    x_hi, y_at, core = elem // 8, (elem // 2) % 4, elem % 2
    return ((x_hi + x) % 2) * 8 + ((y_at + y) % 4) * 2 + (core + c) % 2


def elem_source(elem, step):
    x, y, c = ELEM_STEPS[step]
    x_hi, y_at, core = elem // 8, (elem // 2) % 4, elem % 2
    return ((x_hi + x) % 2) * 8 + ((y_at + 4 - y) % 4) * 2 + (core + c) % 2


def kernel(
    modes_any,
    shapes_any,
    nodes_any,
    natural_any,
    damping_any,
    bins_any,
    phase_any,
    road_any,
    block_any,
    scale_any,
    spectra_ref,
    moments_ref,
    modes,
    shapes,
    nodes,
    natural,
    damping,
    bins,
    phase,
    road,
    block,
    scale,
    picked,
    partial,
    summed,
    wheels,
    factors,
    scaling,
    modal,
    outgoing,
    arrived,
    load_sem,
    send_a,
    recv_a,
    send_b,
    recv_b,
    send_c,
    recv_c,
    send_s,
    recv_s,
):
    elem = lax.axis_index("elem")
    freq = lax.axis_index("freq")
    num_modes = natural.shape[1]
    lines = bins.shape[1]
    width = block.shape[1]
    tiles = -(-num_modes // LANES)
    rows_here = shapes.shape[0]

    barrier = pltpu.get_barrier_semaphore()

    for step in range(PEERS - 1):
        for peer in ((elem, partner(freq, step)), (elem_peer(elem, step), freq)):
            pl.semaphore_signal(barrier, inc=1, device_id=peer, device_id_type=MESH)

    pairs = (
        (shapes_any, shapes),
        (nodes_any, nodes),
        (bins_any, bins),
        (phase_any, phase),
        (road_any, road),
        (natural_any, natural),
        (damping_any, damping),
        (block_any, block),
        (scale_any, scale),
        (modes_any, modes),
    )
    loads = [pltpu.make_async_copy(a, b, load_sem.at[i]) for i, (a, b) in enumerate(pairs)]
    for load in loads:
        load.start()
    for load in loads[:9]:
        load.wait()

    first_row = (elem * PEERS + freq) * rows_here
    row_number = lax.broadcasted_iota(jnp.int32, (rows_here, LANES), 0) + first_row
    masks = [row_number == nodes[:, w : w + 1] for w in range(4)]
    for t in range(tiles):
        lo, hi = t * LANES, min((t + 1) * LANES, num_modes)
        piece = shapes[:, lo:hi]
        found = [
            jnp.sum(jnp.where(m[:, : hi - lo], piece, 0.0), axis=0, keepdims=True) for m in masks
        ]
        picked[t // 2, (t % 2) * 4 : (t % 2) * 4 + 4, : hi - lo] = jnp.concatenate(found, axis=0)
    for j in range((tiles + 1) // 2, PEERS):
        picked[j] = jnp.zeros((8, LANES), jnp.float32)

    ratio = bins[...].astype(jnp.float32) / NBINS
    angle = 2.0 * math.pi / PHASES * phase[...].astype(jnp.float32)
    root = jnp.sqrt(road[...])
    amplitude = jnp.concatenate([root[0:1], root[0:1], root[1:2], root[1:2]], axis=0)
    waves = jnp.concatenate([amplitude * jnp.cos(angle), amplitude * jnp.sin(angle)], axis=0)
    ratios = jnp.concatenate([ratio, jnp.zeros((7, lines), jnp.float32)], axis=0)
    rest = jnp.zeros((8, LANES - 2 * lines), jnp.float32)
    summed[PEERS - 1, 8:] = jnp.concatenate([waves, ratios, rest], axis=1)

    pl.semaphore_wait(barrier, 2 * (PEERS - 1))

    def copy_a(step):
        peer = elem_peer(elem, step)
        return pltpu.make_async_remote_copy(
            src_ref=picked.at[peer],
            dst_ref=partial.at[step],
            send_sem=send_a.at[step],
            recv_sem=recv_a.at[step],
            device_id=(peer, freq),
            device_id_type=MESH,
        )

    def copy_b(step):
        return pltpu.make_async_remote_copy(
            src_ref=summed.at[PEERS - 1],
            dst_ref=summed.at[step],
            send_sem=send_b.at[step],
            recv_sem=recv_b.at[step],
            device_id=(elem, partner(freq, step)),
            device_id_type=MESH,
        )

    def copy_c(step):
        return pltpu.make_async_remote_copy(
            src_ref=wheels.at[elem],
            dst_ref=wheels.at[elem],
            send_sem=send_c.at[step],
            recv_sem=recv_c.at[step],
            device_id=(elem_peer(elem, step), freq),
            device_id_type=MESH,
        )

    def started(copy):
        for step in range(PEERS - 1):
            copy(step).start()

    def received(copy):
        for step in range(PEERS - 1):
            copy(step).wait_recv()

    def sent(copy):
        for step in range(PEERS - 1):
            copy(step).wait_send()

    chunks = (tiles + 1) // 2
    holds = elem < chunks
    for step in range(PEERS - 1):

        @pl.when(elem_peer(elem, step) < chunks)
        def _():
            copy_a(step).start()

    partial[PEERS - 1] = picked[elem]

    sets = block[...]
    found = jnp.zeros(sets.shape, jnp.float32)
    for i in range(scale.shape[1]):
        found = jnp.where(sets == i, scale[:, i : i + 1], found)
    scaling[...] = found
    moments_ref[...] = jnp.zeros(moments_ref.shape, jnp.float32)

    @pl.when(holds)
    def _():
        received(copy_a)

    summed[PEERS - 1, :8] = jnp.sum(partial[...], axis=0)
    started(copy_b)
    received(copy_b)
    wheels[elem] = jnp.sum(summed[:, :8], axis=0)

    @pl.when(holds)
    def _():
        started(copy_c)

    for step in range(PEERS):
        factors[source(freq, step)] = jnp.transpose(summed[step, 8:])[: 2 * lines]
    loads[9].wait()
    for step in range(PEERS - 1):

        @pl.when(elem_source(elem, step) < chunks)
        def _():
            copy_c(step).wait_recv()


    def copy_s(step):
        return pltpu.make_async_remote_copy(
            src_ref=outgoing.at[step],
            dst_ref=arrived.at[step],
            send_sem=send_s.at[step],
            recv_sem=recv_s.at[step],
            device_id=(elem, partner(freq, step)),
            device_id_type=MESH,
        )

    def serve(step, carry):
        table = factors[partner(freq, step)]
        r = table[lines:, 0:1]
        column = [r] + [table[:lines, i : i + 1] for i in range(8)]
        column = [jnp.broadcast_to(c, (lines, LANES)) for c in column]
        square = column[0] * column[0]
        for t in range(tiles):
            lo, hi = t * LANES, min((t + 1) * LANES, num_modes)
            size = hi - lo
            v = natural[:, lo:hi]
            z = damping[:, lo:hi]
            w = [wheels[t // 2, (t % 2) * 4 + i : (t % 2) * 4 + i + 1, :size] for i in range(4)]
            col = [c[:, :size] for c in column]
            own = v * v
            detune = own - square[:, :size]
            damped = (2.0 * z * v) * col[0]
            gain = own / (detune * detune + damped * damped)
            gain_real = gain * detune
            gain_imag = gain * damped
            for k in range(2):
                real = col[1 + 2 * k] * w[2 * k] + col[2 + 2 * k] * w[2 * k + 1]
                imag = col[5 + 2 * k] * w[2 * k] + col[6 + 2 * k] * w[2 * k + 1]
                both = jnp.concatenate(
                    [
                        gain_real * real - gain_imag * imag,
                        -(gain_real * imag + gain_imag * real),
                    ],
                    axis=0,
                )
                modal[2 * k * lines : 2 * (k + 1) * lines, lo:hi] = both.astype(jnp.bfloat16)
        factor = scaling[...]
        stress = []
        for c in range(3):
            product = jnp.dot(modal[...], modes[c], preferred_element_type=jnp.float32) * factor
            stress.append([product[k * lines : (k + 1) * lines] for k in range(4)])

        def real_of(a, b):
            return a[0] * b[0] + a[1] * b[1] + (a[2] * b[2] + a[3] * b[3])

        def imag_of(a, b):
            return a[1] * b[0] - a[0] * b[1] + (a[3] * b[2] - a[2] * b[3])

        def off_real(a, n):
            return a[2] * n[0] - a[3] * n[1] - (a[0] * n[2] - a[1] * n[3])

        def off_imag(a, n):
            return a[2] * n[1] + a[3] * n[0] - (a[0] * n[3] + a[1] * n[2])

        first, second, third = stress
        along, length = unit(first)
        turn, height = unit([off_real(second, along), off_imag(second, along)])
        x, y = off_real(third, along), off_imag(third, along)
        triangle = [
            length,
            real_of(second, along),
            imag_of(second, along),
            real_of(third, along),
            imag_of(third, along),
            height,
            x * turn[0] + y * turn[1],
            y * turn[0] - x * turn[1],
        ]
        for i, value in enumerate(triangle):
            outgoing[step, i] = value.astype(jnp.bfloat16)

        @pl.when(step < PEERS - 1)
        def _():
            copy_s(step).start()

        equivalent = (
            real_of(first, first)
            + real_of(second, second)
            - real_of(first, second)
            + 3.0 * real_of(third, third)
        )
        r2 = r * r
        listed = [
            jnp.sum(value, axis=0, keepdims=True)
            for value in (equivalent, r * equivalent, r2 * equivalent, (r2 * r2) * equivalent)
        ]
        moments_ref[...] += jnp.concatenate(listed, axis=0)
        return carry

    lax.fori_loop(0, PEERS, serve, 0)
    moments_ref[...] = moments_ref[...] / (PEERS * lines)

    def expand(ref, step):
        at = pl.ds(pl.multiple_of(source(freq, step) * width, width), width)
        r, br, bi, cr, ci, h, dr, di = (ref[i].astype(jnp.float32) for i in range(8))
        cross = (
            r * r,
            br * br + bi * bi + h * h,
            cr * cr + ci * ci + (dr * dr + di * di),
            r * br,
            r * cr,
            br * cr + bi * ci + h * dr,
            -(r * bi),
            -(r * ci),
            bi * cr - br * ci - h * di,
        )
        for i, value in enumerate(cross):
            spectra_ref[i, :, at] = value.astype(jnp.bfloat16)

    expand(outgoing.at[PEERS - 1], PEERS - 1)

    def take(step, carry):
        copy_s(step).wait_recv()
        expand(arrived.at[step], step)
        return carry

    lax.fori_loop(0, PEERS - 1, take, 0)
    for step in range(PEERS - 1):

        @pl.when(elem_peer(elem, step) < chunks)
        def _():
            copy_a(step).wait_send()

    @pl.when(holds)
    def _():
        sent(copy_c)

    sent(copy_b)
    sent(copy_s)


def store_kernel(spectra_ref, moments_ref, spectra_out, moments_out, sem):
    copies = [
        pltpu.make_async_copy(spectra_ref.at[i], spectra_out.at[i], sem.at[i])
        for i in range(spectra_ref.shape[0])
    ]
    copies.append(pltpu.make_async_copy(moments_ref, moments_out, sem.at[9]))
    for copy in copies:
        copy.start()
    for copy in copies:
        copy.wait()


def local(*args):
    modes, shapes, nodes, natural, damping, bins, phase, road, block, scale = args
    row = [a.reshape(1, -1) for a in (nodes, natural, damping, bins)]
    args = (modes, shapes, *row, phase, road, block.reshape(1, -1), scale.reshape(1, -1))
    args = [pltpu.with_memory_space_constraint(a, pltpu.HBM) for a in args]
    num_modes, width = modes.shape[1:]
    lines = bins.shape[0]
    f32, bf16 = jnp.float32, jnp.bfloat16
    sems = pltpu.SemaphoreType.DMA((PEERS,))
    spectra, moments = pl.pallas_call(
        kernel,
        out_shape=(
            jax.ShapeDtypeStruct((9, lines, PEERS * width), bf16),
            jax.ShapeDtypeStruct((4, width), f32),
        ),
        in_specs=[pl.BlockSpec(memory_space=pltpu.HBM)] * len(args),
        out_specs=(pl.BlockSpec(memory_space=pltpu.VMEM),) * 2,
        scratch_shapes=[
            *[pltpu.VMEM(a.shape, a.dtype) for a in args],
            pltpu.VMEM((PEERS, 8, LANES), f32),
            pltpu.VMEM((PEERS, 8, LANES), f32),
            pltpu.VMEM((PEERS, 16, LANES), f32),
            pltpu.VMEM((PEERS, 8, LANES), f32),
            pltpu.VMEM((PEERS, 2 * lines, 8), f32),
            pltpu.VMEM((1, width), f32),
            pltpu.VMEM((4 * lines, num_modes), bf16),
            pltpu.VMEM((PEERS, 8, lines, width), bf16),
            pltpu.VMEM((PEERS, 8, lines, width), bf16),
            sems,
            *[sems] * 8,
        ],
        compiler_params=pltpu.CompilerParams(
            collective_id=0, has_side_effects=True, vmem_limit_bytes=40 << 20
        ),
        cost_estimate=pl.CostEstimate(flops=7_100_000_000, bytes_accessed=10_000_000, transcendentals=0),
    )(*args)
    spectra, moments = pl.pallas_call(
        store_kernel,
        out_shape=(
            jax.ShapeDtypeStruct(spectra.shape, spectra.dtype),
            jax.ShapeDtypeStruct(moments.shape, moments.dtype),
        ),
        in_specs=[pl.BlockSpec(memory_space=pltpu.VMEM)] * 2,
        out_specs=[pl.BlockSpec(memory_space=pltpu.HBM)] * 2,
        scratch_shapes=[pltpu.SemaphoreType.DMA((10,))],
    )(*[pltpu.with_memory_space_constraint(a, pltpu.VMEM) for a in (spectra, moments)])
    return jnp.transpose(spectra, (1, 0, 2)), moments


def solution(mesh):
    placed = (
        P(None, None, ("elem", "freq")),
        P(("elem", "freq"), None),
        P(),
        P(),
        P(),
        P("freq"),
        P(None, "freq"),
        P(None, "freq"),
        P(("elem", "freq")),
        P(),
    )
    return jax.shard_map(
        local,
        mesh=mesh,
        in_specs=placed,
        out_specs=(P("freq", None, "elem"), P(None, ("elem", "freq"))),
        check_vma=False,
    )
```

```python
import functools
import math

import jax
import jax.numpy as jnp
from jax import lax
from jax.experimental import pallas as pl
from jax.experimental.pallas import tpu as pltpu
from jax.sharding import PartitionSpec as P

NBINS = 4096
PHASES = 64
LANES = 128
PEERS = 16
MESH = pl.DeviceIdType.MESH


def partner(freq, step):
    across = 1 - step % 2
    rank = step // 2
    odd = rank % 2
    along = odd * (4 - (rank + 1) // 2) + (1 - odd) * (4 + rank // 2)
    x_lo, z = freq // 8, freq % 8
    return ((x_lo + across) % 2) * 8 + (z + along) % 8


def source(freq, step):
    across = 1 - step % 2
    rank = step // 2
    odd = rank % 2
    along = odd * (4 - (rank + 1) // 2) + (1 - odd) * (4 + rank // 2)
    x_lo, z = freq // 8, freq % 8
    return ((x_lo + across) % 2) * 8 + (z + 8 - along) % 8


def unit(parts):
    top = jnp.abs(parts[0])
    for part in parts[1:]:
        top = jnp.maximum(top, jnp.abs(part))
    some = top > 1e-37
    scaled = [part * (1.0 / jnp.where(some, top, 1.0)) for part in parts]
    total = scaled[0] * scaled[0]
    for part in scaled[1:]:
        total += part * part
    shrink = lax.rsqrt(jnp.where(some, total, 1.0))
    direction = [jnp.where(some, part * shrink, 1.0 if i == 0 else 0.0) for i, part in enumerate(scaled)]
    return direction, jnp.where(some, top * (total * shrink), 0.0)


ELEM_STEPS = [(x, y, c) for y in (2, 1, 3, 0) for x in (1, 0) for c in (1, 0)][:-1]


def elem_peer(elem, step):
    x, y, c = ELEM_STEPS[step]
    x_hi, y_at, core = elem // 8, (elem // 2) % 4, elem % 2
    return ((x_hi + x) % 2) * 8 + ((y_at + y) % 4) * 2 + (core + c) % 2


def elem_source(elem, step):
    x, y, c = ELEM_STEPS[step]
    x_hi, y_at, core = elem // 8, (elem // 2) % 4, elem % 2
    return ((x_hi + x) % 2) * 8 + ((y_at + 4 - y) % 4) * 2 + (core + c) % 2


def kernel(
    modes_any,
    shapes_any,
    nodes_any,
    natural_any,
    damping_any,
    bins_any,
    phase_any,
    road_any,
    block_any,
    scale_any,
    spectra_ref,
    moments_ref,
    modes,
    shapes,
    nodes,
    natural,
    damping,
    bins,
    phase,
    road,
    block,
    scale,
    picked,
    partial,
    summed,
    packs,
    wheels,
    factors,
    scaling,
    modal,
    outgoing,
    arrived,
    load_sem,
    send_a,
    recv_a,
    send_b,
    recv_b,
    send_c,
    recv_c,
    send_s,
    recv_s,
    send_f,
    recv_f,
):
    elem = lax.axis_index("elem")
    freq = lax.axis_index("freq")
    num_modes = natural.shape[1]
    lines = bins.shape[1]
    width = block.shape[1]
    tiles = -(-num_modes // LANES)
    rows_here = shapes.shape[0]

    barrier = pltpu.get_barrier_semaphore()

    for step in range(PEERS - 1):
        for peer in ((elem, partner(freq, step)), (elem_peer(elem, step), freq)):
            pl.semaphore_signal(barrier, inc=1, device_id=peer, device_id_type=MESH)

    pairs = (
        (shapes_any, shapes),
        (nodes_any, nodes),
        (bins_any, bins),
        (phase_any, phase),
        (road_any, road),
        (natural_any, natural),
        (damping_any, damping),
        (block_any, block),
        (scale_any, scale),
        (modes_any, modes),
    )
    loads = [pltpu.make_async_copy(a, b, load_sem.at[i]) for i, (a, b) in enumerate(pairs)]
    for load in loads:
        load.start()
    for load in loads[:9]:
        load.wait()

    first_row = (elem * PEERS + freq) * rows_here
    row_number = lax.broadcasted_iota(jnp.int32, (rows_here, LANES), 0) + first_row
    masks = [row_number == nodes[:, w : w + 1] for w in range(4)]
    for t in range(tiles):
        lo, hi = t * LANES, min((t + 1) * LANES, num_modes)
        piece = shapes[:, lo:hi]
        found = [
            jnp.sum(jnp.where(m[:, : hi - lo], piece, 0.0), axis=0, keepdims=True) for m in masks
        ]
        picked[t // 2, (t % 2) * 4 : (t % 2) * 4 + 4, : hi - lo] = jnp.concatenate(found, axis=0)
    for j in range((tiles + 1) // 2, PEERS):
        picked[j] = jnp.zeros((8, LANES), jnp.float32)

    ratio = bins[...].astype(jnp.float32) / NBINS
    angle = 2.0 * math.pi / PHASES * phase[...].astype(jnp.float32)
    root = jnp.sqrt(road[...])
    amplitude = jnp.concatenate([root[0:1], root[0:1], root[1:2], root[1:2]], axis=0)
    waves = jnp.concatenate([amplitude * jnp.cos(angle), amplitude * jnp.sin(angle)], axis=0)
    ratios = jnp.concatenate([ratio, jnp.zeros((7, lines), jnp.float32)], axis=0)
    rest = jnp.zeros((8, LANES - 2 * lines), jnp.float32)
    packs[PEERS - 1] = jnp.concatenate([waves, ratios, rest], axis=1)

    pl.semaphore_wait(barrier, 2 * (PEERS - 1))

    def copy_a(step):
        peer = elem_peer(elem, step)
        return pltpu.make_async_remote_copy(
            src_ref=picked.at[peer],
            dst_ref=partial.at[step],
            send_sem=send_a.at[step],
            recv_sem=recv_a.at[step],
            device_id=(peer, freq),
            device_id_type=MESH,
        )

    def copy_f(step):
        return pltpu.make_async_remote_copy(
            src_ref=packs.at[PEERS - 1],
            dst_ref=packs.at[step],
            send_sem=send_f.at[step],
            recv_sem=recv_f.at[step],
            device_id=(elem, partner(freq, step)),
            device_id_type=MESH,
        )

    def copy_b(step):
        return pltpu.make_async_remote_copy(
            src_ref=summed.at[PEERS - 1],
            dst_ref=summed.at[step],
            send_sem=send_b.at[step],
            recv_sem=recv_b.at[step],
            device_id=(elem, partner(freq, step)),
            device_id_type=MESH,
        )

    def copy_c(step):
        return pltpu.make_async_remote_copy(
            src_ref=wheels.at[elem],
            dst_ref=wheels.at[elem],
            send_sem=send_c.at[step],
            recv_sem=recv_c.at[step],
            device_id=(elem_peer(elem, step), freq),
            device_id_type=MESH,
        )

    def started(copy):
        for step in range(PEERS - 1):
            copy(step).start()

    def received(copy):
        for step in range(PEERS - 1):
            copy(step).wait_recv()

    def sent(copy):
        for step in range(PEERS - 1):
            copy(step).wait_send()

    chunks = (tiles + 1) // 2
    holds = elem < chunks
    for step in range(PEERS - 1):

        @pl.when(elem_peer(elem, step) < chunks)
        def _():
            copy_a(step).start()

    started(copy_f)
    partial[PEERS - 1] = picked[elem]

    sets = block[...]
    found = jnp.zeros(sets.shape, jnp.float32)
    for i in range(scale.shape[1]):
        found = jnp.where(sets == i, scale[:, i : i + 1], found)
    scaling[...] = found
    moments_ref[...] = jnp.zeros(moments_ref.shape, jnp.float32)

    @pl.when(holds)
    def _():
        received(copy_a)
        summed[PEERS - 1] = jnp.sum(partial[...], axis=0)
        started(copy_b)
        received(copy_b)
        wheels[elem] = jnp.sum(summed[...], axis=0)
        started(copy_c)

    received(copy_f)
    for step in range(PEERS):
        factors[source(freq, step)] = jnp.transpose(packs[step])[: 2 * lines]
    loads[9].wait()
    for step in range(PEERS - 1):

        @pl.when(elem_source(elem, step) < chunks)
        def _():
            copy_c(step).wait_recv()


    def copy_s(step):
        return pltpu.make_async_remote_copy(
            src_ref=outgoing.at[step],
            dst_ref=arrived.at[step],
            send_sem=send_s.at[step],
            recv_sem=recv_s.at[step],
            device_id=(elem, partner(freq, step)),
            device_id_type=MESH,
        )

    def serve(step, carry):
        table = factors[partner(freq, step)]
        r = table[lines:, 0:1]
        column = [r] + [table[:lines, i : i + 1] for i in range(8)]
        column = [jnp.broadcast_to(c, (lines, LANES)) for c in column]
        square = column[0] * column[0]
        for t in range(tiles):
            lo, hi = t * LANES, min((t + 1) * LANES, num_modes)
            size = hi - lo
            v = natural[:, lo:hi]
            z = damping[:, lo:hi]
            w = [wheels[t // 2, (t % 2) * 4 + i : (t % 2) * 4 + i + 1, :size] for i in range(4)]
            col = [c[:, :size] for c in column]
            own = v * v
            detune = own - square[:, :size]
            damped = (2.0 * z * v) * col[0]
            gain = own / (detune * detune + damped * damped)
            gain_real = gain * detune
            gain_imag = gain * damped
            for k in range(2):
                real = col[1 + 2 * k] * w[2 * k] + col[2 + 2 * k] * w[2 * k + 1]
                imag = col[5 + 2 * k] * w[2 * k] + col[6 + 2 * k] * w[2 * k + 1]
                both = jnp.concatenate(
                    [
                        gain_real * real - gain_imag * imag,
                        -(gain_real * imag + gain_imag * real),
                    ],
                    axis=0,
                )
                modal[2 * k * lines : 2 * (k + 1) * lines, lo:hi] = both.astype(jnp.bfloat16)
        factor = scaling[...]
        stress = []
        for c in range(3):
            product = jnp.dot(modal[...], modes[c], preferred_element_type=jnp.float32) * factor
            stress.append([product[k * lines : (k + 1) * lines] for k in range(4)])

        def real_of(a, b):
            return a[0] * b[0] + a[1] * b[1] + (a[2] * b[2] + a[3] * b[3])

        def imag_of(a, b):
            return a[1] * b[0] - a[0] * b[1] + (a[3] * b[2] - a[2] * b[3])

        def off_real(a, n):
            return a[2] * n[0] - a[3] * n[1] - (a[0] * n[2] - a[1] * n[3])

        def off_imag(a, n):
            return a[2] * n[1] + a[3] * n[0] - (a[0] * n[3] + a[1] * n[2])

        first, second, third = stress
        along, length = unit(first)
        turn, height = unit([off_real(second, along), off_imag(second, along)])
        x, y = off_real(third, along), off_imag(third, along)
        triangle = [
            length,
            real_of(second, along),
            imag_of(second, along),
            real_of(third, along),
            imag_of(third, along),
            height,
            x * turn[0] + y * turn[1],
            y * turn[0] - x * turn[1],
        ]
        for i, value in enumerate(triangle):
            outgoing[step, i] = value.astype(jnp.bfloat16)

        @pl.when(step < PEERS - 1)
        def _():
            copy_s(step).start()

        equivalent = (
            real_of(first, first)
            + real_of(second, second)
            - real_of(first, second)
            + 3.0 * real_of(third, third)
        )
        r2 = r * r
        listed = [
            jnp.sum(value, axis=0, keepdims=True)
            for value in (equivalent, r * equivalent, r2 * equivalent, (r2 * r2) * equivalent)
        ]
        moments_ref[...] += jnp.concatenate(listed, axis=0)
        return carry

    lax.fori_loop(0, PEERS, serve, 0)
    moments_ref[...] = moments_ref[...] / (PEERS * lines)

    def expand(ref, step):
        at = pl.ds(pl.multiple_of(source(freq, step) * width, width), width)
        r, br, bi, cr, ci, h, dr, di = (ref[i].astype(jnp.float32) for i in range(8))
        cross = (
            r * r,
            br * br + bi * bi + h * h,
            cr * cr + ci * ci + (dr * dr + di * di),
            r * br,
            r * cr,
            br * cr + bi * ci + h * dr,
            -(r * bi),
            -(r * ci),
            bi * cr - br * ci - h * di,
        )
        for i, value in enumerate(cross):
            spectra_ref[i, :, at] = value.astype(jnp.bfloat16)

    expand(outgoing.at[PEERS - 1], PEERS - 1)

    def take(step, carry):
        copy_s(step).wait_recv()
        expand(arrived.at[step], step)
        return carry

    lax.fori_loop(0, PEERS - 1, take, 0)
    for step in range(PEERS - 1):

        @pl.when(elem_peer(elem, step) < chunks)
        def _():
            copy_a(step).wait_send()

    @pl.when(holds)
    def _():
        sent(copy_b)
        sent(copy_c)

    sent(copy_f)
    sent(copy_s)


def store_kernel(spectra_ref, moments_ref, spectra_out, moments_out, sem):
    copies = [
        pltpu.make_async_copy(spectra_ref.at[i], spectra_out.at[i], sem.at[i])
        for i in range(spectra_ref.shape[0])
    ]
    copies.append(pltpu.make_async_copy(moments_ref, moments_out, sem.at[9]))
    for copy in copies:
        copy.start()
    for copy in copies:
        copy.wait()


def local(*args):
    modes, shapes, nodes, natural, damping, bins, phase, road, block, scale = args
    row = [a.reshape(1, -1) for a in (nodes, natural, damping, bins)]
    args = (modes, shapes, *row, phase, road, block.reshape(1, -1), scale.reshape(1, -1))
    args = [pltpu.with_memory_space_constraint(a, pltpu.HBM) for a in args]
    num_modes, width = modes.shape[1:]
    lines = bins.shape[0]
    f32, bf16 = jnp.float32, jnp.bfloat16
    sems = pltpu.SemaphoreType.DMA((PEERS,))
    spectra, moments = pl.pallas_call(
        kernel,
        out_shape=(
            jax.ShapeDtypeStruct((9, lines, PEERS * width), bf16),
            jax.ShapeDtypeStruct((4, width), f32),
        ),
        in_specs=[pl.BlockSpec(memory_space=pltpu.HBM)] * len(args),
        out_specs=(pl.BlockSpec(memory_space=pltpu.VMEM),) * 2,
        scratch_shapes=[
            *[pltpu.VMEM(a.shape, a.dtype) for a in args],
            pltpu.VMEM((PEERS, 8, LANES), f32),
            pltpu.VMEM((PEERS, 8, LANES), f32),
            pltpu.VMEM((PEERS, 8, LANES), f32),
            pltpu.VMEM((PEERS, 8, LANES), f32),
            pltpu.VMEM((PEERS, 8, LANES), f32),
            pltpu.VMEM((PEERS, 2 * lines, 8), f32),
            pltpu.VMEM((1, width), f32),
            pltpu.VMEM((4 * lines, num_modes), bf16),
            pltpu.VMEM((PEERS, 8, lines, width), bf16),
            pltpu.VMEM((PEERS, 8, lines, width), bf16),
            sems,
            *[sems] * 10,
        ],
        compiler_params=pltpu.CompilerParams(
            collective_id=0, has_side_effects=True, vmem_limit_bytes=40 << 20
        ),
        cost_estimate=pl.CostEstimate(flops=7_100_000_000, bytes_accessed=10_000_000, transcendentals=0),
    )(*args)
    spectra, moments = pl.pallas_call(
        store_kernel,
        out_shape=(
            jax.ShapeDtypeStruct(spectra.shape, spectra.dtype),
            jax.ShapeDtypeStruct(moments.shape, moments.dtype),
        ),
        in_specs=[pl.BlockSpec(memory_space=pltpu.VMEM)] * 2,
        out_specs=[pl.BlockSpec(memory_space=pltpu.HBM)] * 2,
        scratch_shapes=[pltpu.SemaphoreType.DMA((10,))],
    )(*[pltpu.with_memory_space_constraint(a, pltpu.VMEM) for a in (spectra, moments)])
    return jnp.transpose(spectra, (1, 0, 2)), moments


def solution(mesh):
    placed = (
        P(None, None, ("elem", "freq")),
        P(("elem", "freq"), None),
        P(),
        P(),
        P(),
        P("freq"),
        P(None, "freq"),
        P(None, "freq"),
        P(("elem", "freq")),
        P(),
    )
    return jax.shard_map(
        local,
        mesh=mesh,
        in_specs=placed,
        out_specs=(P("freq", None, "elem"), P(None, ("elem", "freq"))),
        check_vma=False,
    )
```

```python
import functools
import math

import jax
import jax.numpy as jnp
from jax import lax
from jax.experimental import pallas as pl
from jax.experimental.pallas import tpu as pltpu
from jax.sharding import PartitionSpec as P

NBINS = 4096
PHASES = 64
LANES = 128
PEERS = 16
MESH = pl.DeviceIdType.MESH


def partner(freq, step):
    across = 1 - step % 2
    rank = step // 2
    odd = rank % 2
    along = odd * (4 - (rank + 1) // 2) + (1 - odd) * (4 + rank // 2)
    x_lo, z = freq // 8, freq % 8
    return ((x_lo + across) % 2) * 8 + (z + along) % 8


def source(freq, step):
    across = 1 - step % 2
    rank = step // 2
    odd = rank % 2
    along = odd * (4 - (rank + 1) // 2) + (1 - odd) * (4 + rank // 2)
    x_lo, z = freq // 8, freq % 8
    return ((x_lo + across) % 2) * 8 + (z + 8 - along) % 8


def unit(parts):
    top = jnp.abs(parts[0])
    for part in parts[1:]:
        top = jnp.maximum(top, jnp.abs(part))
    some = top > 1e-37
    scaled = [part * (1.0 / jnp.where(some, top, 1.0)) for part in parts]
    total = scaled[0] * scaled[0]
    for part in scaled[1:]:
        total += part * part
    shrink = lax.rsqrt(jnp.where(some, total, 1.0))
    direction = [jnp.where(some, part * shrink, 1.0 if i == 0 else 0.0) for i, part in enumerate(scaled)]
    return direction, jnp.where(some, top * (total * shrink), 0.0)


ELEM_STEPS = [(x, y, c) for y in (2, 1, 3, 0) for x in (1, 0) for c in (1, 0)][:-1]


def elem_peer(elem, step):
    x, y, c = ELEM_STEPS[step]
    x_hi, y_at, core = elem // 8, (elem // 2) % 4, elem % 2
    return ((x_hi + x) % 2) * 8 + ((y_at + y) % 4) * 2 + (core + c) % 2


def elem_source(elem, step):
    x, y, c = ELEM_STEPS[step]
    x_hi, y_at, core = elem // 8, (elem // 2) % 4, elem % 2
    return ((x_hi + x) % 2) * 8 + ((y_at + 4 - y) % 4) * 2 + (core + c) % 2


def kernel(
    modes_any,
    shapes_any,
    nodes_any,
    natural_any,
    damping_any,
    bins_any,
    phase_any,
    road_any,
    block_any,
    scale_any,
    spectra_ref,
    moments_ref,
    modes,
    shapes,
    nodes,
    natural,
    damping,
    bins,
    phase,
    road,
    block,
    scale,
    picked,
    partial,
    summed,
    packs,
    wheels,
    factors,
    scaling,
    modal,
    outgoing,
    arrived,
    load_sem,
    send_a,
    recv_a,
    send_b,
    recv_b,
    send_c,
    recv_c,
    send_s,
    recv_s,
    send_f,
    recv_f,
):
    elem = lax.axis_index("elem")
    freq = lax.axis_index("freq")
    num_modes = natural.shape[1]
    lines = bins.shape[1]
    width = block.shape[1]
    tiles = -(-num_modes // LANES)
    rows_here = shapes.shape[0]

    barrier = pltpu.get_barrier_semaphore()

    for step in range(PEERS - 1):
        for peer in ((elem, partner(freq, step)), (elem_peer(elem, step), freq)):
            pl.semaphore_signal(barrier, inc=1, device_id=peer, device_id_type=MESH)

    pairs = (
        (shapes_any, shapes),
        (nodes_any, nodes),
        (bins_any, bins),
        (phase_any, phase),
        (road_any, road),
        (natural_any, natural),
        (damping_any, damping),
        (block_any, block),
        (scale_any, scale),
        (modes_any, modes),
    )
    loads = [pltpu.make_async_copy(a, b, load_sem.at[i]) for i, (a, b) in enumerate(pairs)]
    for load in loads:
        load.start()
    for load in loads[:9]:
        load.wait()

    first_row = (elem * PEERS + freq) * rows_here
    row_number = lax.broadcasted_iota(jnp.int32, (rows_here, LANES), 0) + first_row
    masks = [row_number == nodes[:, w : w + 1] for w in range(4)]
    for t in range(tiles):
        lo, hi = t * LANES, min((t + 1) * LANES, num_modes)
        piece = shapes[:, lo:hi]
        found = [
            jnp.sum(jnp.where(m[:, : hi - lo], piece, 0.0), axis=0, keepdims=True) for m in masks
        ]
        picked[t // 2, (t % 2) * 4 : (t % 2) * 4 + 4, : hi - lo] = jnp.concatenate(found, axis=0)
    for j in range((tiles + 1) // 2, PEERS):
        picked[j] = jnp.zeros((8, LANES), jnp.float32)

    ratio = bins[...].astype(jnp.float32) / NBINS
    angle = 2.0 * math.pi / PHASES * phase[...].astype(jnp.float32)
    root = jnp.sqrt(road[...])
    amplitude = jnp.concatenate([root[0:1], root[0:1], root[1:2], root[1:2]], axis=0)
    waves = jnp.concatenate([amplitude * jnp.cos(angle), amplitude * jnp.sin(angle)], axis=0)
    ratios = jnp.concatenate([ratio, jnp.zeros((7, lines), jnp.float32)], axis=0)
    rest = jnp.zeros((8, LANES - 2 * lines), jnp.float32)
    packs[PEERS - 1] = jnp.concatenate([waves, ratios, rest], axis=1)

    pl.semaphore_wait(barrier, 2 * (PEERS - 1))

    def copy_a(step):
        peer = elem_peer(elem, step)
        return pltpu.make_async_remote_copy(
            src_ref=picked.at[peer],
            dst_ref=partial.at[step],
            send_sem=send_a.at[step],
            recv_sem=recv_a.at[step],
            device_id=(peer, freq),
            device_id_type=MESH,
        )

    def copy_f(step):
        return pltpu.make_async_remote_copy(
            src_ref=packs.at[PEERS - 1],
            dst_ref=packs.at[step],
            send_sem=send_f.at[step],
            recv_sem=recv_f.at[step],
            device_id=(elem, partner(freq, step)),
            device_id_type=MESH,
        )

    def copy_b(step):
        return pltpu.make_async_remote_copy(
            src_ref=summed.at[PEERS - 1],
            dst_ref=summed.at[step],
            send_sem=send_b.at[step],
            recv_sem=recv_b.at[step],
            device_id=(elem, partner(freq, step)),
            device_id_type=MESH,
        )

    def copy_c(step):
        return pltpu.make_async_remote_copy(
            src_ref=wheels.at[elem],
            dst_ref=wheels.at[elem],
            send_sem=send_c.at[step],
            recv_sem=recv_c.at[step],
            device_id=(elem_peer(elem, step), freq),
            device_id_type=MESH,
        )

    def started(copy):
        for step in range(PEERS - 1):
            copy(step).start()

    def received(copy):
        for step in range(PEERS - 1):
            copy(step).wait_recv()

    def sent(copy):
        for step in range(PEERS - 1):
            copy(step).wait_send()

    chunks = (tiles + 1) // 2
    holds = elem < chunks
    for step in range(PEERS - 1):

        @pl.when(elem_peer(elem, step) < chunks)
        def _():
            copy_a(step).start()

    started(copy_f)
    partial[PEERS - 1] = picked[elem]

    sets = block[...]
    found = jnp.zeros(sets.shape, jnp.float32)
    for i in range(scale.shape[1]):
        found = jnp.where(sets == i, scale[:, i : i + 1], found)
    scaling[...] = found
    moments_ref[...] = jnp.zeros(moments_ref.shape, jnp.float32)

    @pl.when(holds)
    def _():
        received(copy_a)
        summed[PEERS - 1] = jnp.sum(partial[...], axis=0)
        started(copy_b)
        received(copy_b)
        wheels[elem] = jnp.sum(summed[...], axis=0)
        started(copy_c)

    received(copy_f)
    for step in range(PEERS):
        factors[source(freq, step)] = jnp.transpose(packs[step])[: 2 * lines]
    loads[9].wait()
    for step in range(PEERS - 1):

        @pl.when(elem_source(elem, step) < chunks)
        def _():
            copy_c(step).wait_recv()


    def copy_s(step):
        return pltpu.make_async_remote_copy(
            src_ref=outgoing.at[step],
            dst_ref=arrived.at[step],
            send_sem=send_s.at[step],
            recv_sem=recv_s.at[step],
            device_id=(elem, partner(freq, step)),
            device_id_type=MESH,
        )

    def serve(step, carry):
        table = factors[partner(freq, step)]
        r = table[lines:, 0:1]
        column = [r] + [table[:lines, i : i + 1] for i in range(8)]
        column = [jnp.broadcast_to(c, (lines, LANES)) for c in column]
        square = column[0] * column[0]
        for t in range(tiles):
            lo, hi = t * LANES, min((t + 1) * LANES, num_modes)
            size = hi - lo
            v = natural[:, lo:hi]
            z = damping[:, lo:hi]
            w = [wheels[t // 2, (t % 2) * 4 + i : (t % 2) * 4 + i + 1, :size] for i in range(4)]
            col = [c[:, :size] for c in column]
            own = v * v
            detune = own - square[:, :size]
            damped = (2.0 * z * v) * col[0]
            gain = own / (detune * detune + damped * damped)
            gain_real = gain * detune
            gain_imag = gain * damped
            for k in range(2):
                real = col[1 + 2 * k] * w[2 * k] + col[2 + 2 * k] * w[2 * k + 1]
                imag = col[5 + 2 * k] * w[2 * k] + col[6 + 2 * k] * w[2 * k + 1]
                both = jnp.concatenate(
                    [
                        gain_real * real - gain_imag * imag,
                        -(gain_real * imag + gain_imag * real),
                    ],
                    axis=0,
                )
                modal[2 * k * lines : 2 * (k + 1) * lines, lo:hi] = both.astype(jnp.bfloat16)
        factor = scaling[...]
        stress = []
        for c in range(3):
            product = jnp.dot(modal[...], modes[c], preferred_element_type=jnp.float32) * factor
            stress.append([product[k * lines : (k + 1) * lines] for k in range(4)])

        def real_of(a, b):
            return a[0] * b[0] + a[1] * b[1] + (a[2] * b[2] + a[3] * b[3])

        def imag_of(a, b):
            return a[1] * b[0] - a[0] * b[1] + (a[3] * b[2] - a[2] * b[3])

        def off_real(a, n):
            return a[2] * n[0] - a[3] * n[1] - (a[0] * n[2] - a[1] * n[3])

        def off_imag(a, n):
            return a[2] * n[1] + a[3] * n[0] - (a[0] * n[3] + a[1] * n[2])

        first, second, third = stress
        along, length = unit(first)
        turn, height = unit([off_real(second, along), off_imag(second, along)])
        x, y = off_real(third, along), off_imag(third, along)
        triangle = [
            length,
            real_of(second, along),
            imag_of(second, along),
            real_of(third, along),
            imag_of(third, along),
            height,
            x * turn[0] + y * turn[1],
            y * turn[0] - x * turn[1],
        ]
        for i, value in enumerate(triangle):
            outgoing[step, i] = value.astype(jnp.bfloat16)

        @pl.when(step < PEERS - 1)
        def _():
            copy_s(step).start()

        equivalent = (
            real_of(first, first)
            + real_of(second, second)
            - real_of(first, second)
            + 3.0 * real_of(third, third)
        )
        r2 = r * r
        listed = [
            jnp.sum(value, axis=0, keepdims=True)
            for value in (equivalent, r * equivalent, r2 * equivalent, (r2 * r2) * equivalent)
        ]
        moments_ref[...] += jnp.concatenate(listed, axis=0)
        return carry

    lax.fori_loop(0, PEERS, serve, 0)
    moments_ref[...] = moments_ref[...] / (PEERS * lines)

    def expand(ref, step):
        at = pl.ds(pl.multiple_of(source(freq, step) * width, width), width)
        r, br, bi, cr, ci, h, dr, di = (ref[i].astype(jnp.float32) for i in range(8))
        cross = (
            r * r,
            br * br + bi * bi + h * h,
            cr * cr + ci * ci + (dr * dr + di * di),
            r * br,
            r * cr,
            br * cr + bi * ci + h * dr,
            -(r * bi),
            -(r * ci),
            bi * cr - br * ci - h * di,
        )
        for i, value in enumerate(cross):
            spectra_ref[i, :, at] = value.astype(jnp.bfloat16)

    expand(outgoing.at[PEERS - 1], PEERS - 1)

    def take(step, carry):
        copy_s(step).wait_recv()
        expand(arrived.at[step], step)
        return carry

    lax.fori_loop(0, PEERS - 1, take, 0)
    for step in range(PEERS - 1):

        @pl.when(elem_peer(elem, step) < chunks)
        def _():
            copy_a(step).wait_send()

    @pl.when(holds)
    def _():
        sent(copy_b)
        sent(copy_c)

    sent(copy_f)
    sent(copy_s)


def store_kernel(spectra_ref, moments_ref, spectra_out, moments_out, sem):
    copies = [
        pltpu.make_async_copy(
            spectra_ref.at[pl.ds(3 * i, 3)], spectra_out.at[pl.ds(3 * i, 3)], sem.at[i]
        )
        for i in range(spectra_ref.shape[0] // 3)
    ]
    copies.append(pltpu.make_async_copy(moments_ref, moments_out, sem.at[9]))
    for copy in copies:
        copy.start()
    for copy in copies:
        copy.wait()


def local(*args):
    modes, shapes, nodes, natural, damping, bins, phase, road, block, scale = args
    row = [a.reshape(1, -1) for a in (nodes, natural, damping, bins)]
    args = (modes, shapes, *row, phase, road, block.reshape(1, -1), scale.reshape(1, -1))
    args = [pltpu.with_memory_space_constraint(a, pltpu.HBM) for a in args]
    num_modes, width = modes.shape[1:]
    lines = bins.shape[0]
    f32, bf16 = jnp.float32, jnp.bfloat16
    sems = pltpu.SemaphoreType.DMA((PEERS,))
    spectra, moments = pl.pallas_call(
        kernel,
        out_shape=(
            jax.ShapeDtypeStruct((9, lines, PEERS * width), bf16),
            jax.ShapeDtypeStruct((4, width), f32),
        ),
        in_specs=[pl.BlockSpec(memory_space=pltpu.HBM)] * len(args),
        out_specs=(pl.BlockSpec(memory_space=pltpu.VMEM),) * 2,
        scratch_shapes=[
            *[pltpu.VMEM(a.shape, a.dtype) for a in args],
            pltpu.VMEM((PEERS, 8, LANES), f32),
            pltpu.VMEM((PEERS, 8, LANES), f32),
            pltpu.VMEM((PEERS, 8, LANES), f32),
            pltpu.VMEM((PEERS, 8, LANES), f32),
            pltpu.VMEM((PEERS, 8, LANES), f32),
            pltpu.VMEM((PEERS, 2 * lines, 8), f32),
            pltpu.VMEM((1, width), f32),
            pltpu.VMEM((4 * lines, num_modes), bf16),
            pltpu.VMEM((PEERS, 8, lines, width), bf16),
            pltpu.VMEM((PEERS, 8, lines, width), bf16),
            sems,
            *[sems] * 10,
        ],
        compiler_params=pltpu.CompilerParams(
            collective_id=0, has_side_effects=True, vmem_limit_bytes=40 << 20
        ),
        cost_estimate=pl.CostEstimate(flops=7_100_000_000, bytes_accessed=10_000_000, transcendentals=0),
    )(*args)
    spectra, moments = pl.pallas_call(
        store_kernel,
        out_shape=(
            jax.ShapeDtypeStruct(spectra.shape, spectra.dtype),
            jax.ShapeDtypeStruct(moments.shape, moments.dtype),
        ),
        in_specs=[pl.BlockSpec(memory_space=pltpu.VMEM)] * 2,
        out_specs=[pl.BlockSpec(memory_space=pltpu.HBM)] * 2,
        scratch_shapes=[pltpu.SemaphoreType.DMA((10,))],
    )(*[pltpu.with_memory_space_constraint(a, pltpu.VMEM) for a in (spectra, moments)])
    return jnp.transpose(spectra, (1, 0, 2)), moments


def solution(mesh):
    placed = (
        P(None, None, ("elem", "freq")),
        P(("elem", "freq"), None),
        P(),
        P(),
        P(),
        P("freq"),
        P(None, "freq"),
        P(None, "freq"),
        P(("elem", "freq")),
        P(),
    )
    return jax.shard_map(
        local,
        mesh=mesh,
        in_specs=placed,
        out_specs=(P("freq", None, "elem"), P(None, ("elem", "freq"))),
        check_vma=False,
    )
```
